32 devices in a mesh: row: 8 (over z, x), col: 4 (over y, core).
Axes of the slice: x: 2, y: 2, z: 4, core: 2. Of those that a mesh axis runs over, the one named last changes fastest.
Arguments:
- panels: int32 [1], replicated, may hold values from 0 to 15
- inverse: float32 [16384, 16384], P('row', 'col'), may hold values from -4 to 28, as said below
- weight: float32 [1024, 16384], P('row', 'col'), may hold values from -0.046875 to 0.046875
- tokens: bfloat16 [1024, 16384], P('row', 'col'), may hold values from -6 to 6
- targets: bfloat16 [1024, 1024], P('row', 'col'), may hold values from -6 to 6
Outputs:
- new_inverse: float32 [16384, 16384], P('row', 'col')
- pruned: float32 [1024, 16384], P('row', 'col')
- residual: float32 [1024, 1024], P('row', 'col')
- correlation: float32 [1024, 16384], P('row', 'col')
The draws below stay inside these ranges and needn't reach their ends.
Inputs may be any that keep to these rules, and one draw needn't show every extreme that they name: `inverse`: symmetric and positive definite.
All inputs are finite; a program needn't handle non-finite values.
Results may differ from the reference program's by a relative error of at most 0.0035.
Values may be sent and summed in bfloat16 or wider, within the bound.
No kernel may reach another device: no remote copies, remote signals or barrier semaphores. Data moves between devices by JAX's collectives and lax.ppermute only.
A program may use at most 192 MiB of HBM per device.

```python
import math
import jax
import jax.numpy as jnp
from jax import lax

D = 16384
PW = 1024
OUT = 1024
ROUNDS = 1
TOKENS = 1024


def draw_inverse(key, part):
    key_noise = jax.random.fold_in(key, 11)
    key_diag = jax.random.fold_in(key, 12)
    key_coupling = jax.random.fold_in(key, 14)
    key_signs = jax.random.fold_in(key, 15)
    gaussian = jnp.clip(jax.random.normal(key_noise, (D, D), jnp.float32), -6.0, 6.0)
    symmetric = (gaussian + gaussian.T) * (0.5 / math.sqrt(2.0 * D))
    diagonal = jax.random.uniform(key_diag, (D,), jnp.float32, 1.5, 3.0)
    coupling = jnp.exp(jax.random.uniform(key_coupling, (D,), jnp.float32, math.log(0.5), math.log(2.0)))
    reach_length = max(PW / 32.0, 2.0)
    position = jnp.arange(D, dtype=jnp.float32)
    distance = jnp.abs(position[:, None] - position[None, :])
    kernel = 0.25 * jnp.exp(-distance / reach_length) * coupling[:, None] * coupling[None, :]
    inner_width = D // 16
    signs = jnp.where(jax.random.bernoulli(key_signs, 0.5, (D, inner_width)), 1.0, -1.0).astype(jnp.float32)
    gram = jnp.dot(signs, signs.T, precision=lax.Precision.HIGHEST, preferred_element_type=jnp.float32) * (1.0 / inner_width)
    matrix = kernel + symmetric + gram + jnp.diag(diagonal)
    return matrix.astype(jnp.float32)


def steps_of(own_key, dims, cuts, smallest, top_value):
    gain, own = 1.0, jax.random.fold_in(own_key, 6)
    for dim, blocks in cuts:
        heights = jnp.exp(jax.random.uniform(jax.random.fold_in(own, dim), (blocks,), jnp.float32, smallest / len(cuts), top_value / len(cuts)))
        gain = gain * jnp.repeat(heights, dims[dim] // blocks).reshape([-1 if axis == dim else 1 for axis in range(len(dims))])
    return gain


def centred(rng, dims, width, reach, split=(), held_as=jnp.bfloat16):
    array = jax.random.normal(rng, dims, jnp.float32) * width
    if len(split) > 0:
        array = steps_of(rng, dims, split, -0.22, 0.18) * array
    return jnp.clip(array, min=-reach, max=reach).astype(held_as)


def setup_inputs(seed: int = 0) -> dict:
    key_list = jax.random.split(jax.random.key(seed), 6)
    panels = jax.random.randint(key_list[0], (ROUNDS,), 0, D // PW).astype(jnp.int32)
    inverse = draw_inverse(jax.random.fold_in(key_list[5], 71), 0)
    weight = centred(key_list[2], (OUT, D), D ** -0.5, 0.046875, ((0, 8), (1, 4)), jnp.float32)
    tokens = centred(key_list[3], (TOKENS, D), 1.0, 6.0, ((0, 8), (1, 4)))
    targets = centred(key_list[4], (TOKENS, OUT), 1.0, 6.0, ((0, 8), (1, 4)))
    return {"panels": panels, "inverse": inverse, "weight": weight, "tokens": tokens, "targets": targets}


def reference(panels, inverse, weight, tokens, targets):
    highest = lax.Precision.HIGHEST
    anchor = (panels[0] * PW).astype(jnp.int32)
    column = lax.dynamic_slice_in_dim(inverse, anchor, PW, 1)
    row_panel = lax.dynamic_slice_in_dim(inverse, anchor, PW, 0)
    diag_block = lax.dynamic_slice_in_dim(row_panel, anchor, PW, 1)
    factor = jnp.linalg.cholesky(diag_block)
    halfway = lax.linalg.triangular_solve(factor, row_panel, left_side=True, lower=True, transpose_a=False)
    solved = lax.linalg.triangular_solve(factor, halfway, left_side=True, lower=True, transpose_a=True)
    new_inverse = inverse - jnp.dot(column.astype(jnp.float32), solved.astype(jnp.float32), precision=highest, preferred_element_type=jnp.float32)
    weight_cols = lax.dynamic_slice_in_dim(weight, anchor, PW, 1)
    pruned = weight - jnp.dot(weight_cols.astype(jnp.float32), solved.astype(jnp.float32), precision=highest, preferred_element_type=jnp.float32)
    pruned_low = pruned.astype(jnp.bfloat16)
    residual = jnp.dot(tokens.astype(jnp.float32), pruned_low.T.astype(jnp.float32), preferred_element_type=jnp.float32) - targets.astype(jnp.float32)
    residual_low = residual.astype(jnp.bfloat16)
    correlation = jnp.dot(residual_low.T.astype(jnp.float32), tokens.astype(jnp.float32), preferred_element_type=jnp.float32) * (1.0 / math.sqrt(TOKENS))
    return (new_inverse, pruned, residual, correlation)
```

```python
import functools
import math

import jax
import jax.numpy as jnp
from jax import lax
from jax.experimental import pallas as pl
from jax.experimental.pallas import tpu as pltpu
from jax.sharding import PartitionSpec as P

PW = 1024
TILE = 256
NB = 128
CHUNKS = 4

BF16 = jnp.bfloat16
F32 = jnp.float32


def bits(n):
    return [1 << b for b in range(n.bit_length() - 1)]


def swap(x, axis, bit):
    n = lax.axis_size(axis)
    return lax.ppermute(x, axis, [(i, i ^ bit) for i in range(n)])


def joint(pairs, cols):
    return [(a * cols + c, b * cols + d) for (a, c), (b, d) in pairs]


def pick(cond, a, b):
    return jnp.where(cond, a, b), jnp.where(cond, b, a)


def scatter_step(x, bit, root):
    col = lax.axis_index("col")
    low = (col & bit) == 0
    mine, other = pick(low, x[0::2], x[1::2])
    got = swap(other, "col", bit)
    return jnp.where(((col ^ root) & bit) == 0, mine, got)


def gather_step(x, bit):
    low = (lax.axis_index("col") & bit) == 0
    got = swap(x, "col", bit)
    a, b = pick(low, x, got)
    return jnp.stack([a, b], 1).reshape((2 * x.shape[0],) + x.shape[1:])


def spread_step(x, axis, bit, root):
    got = swap(x, axis, bit)
    return jnp.where(((lax.axis_index(axis) ^ root) & bit) == 0, x, got)


def spread_block(block, owner_row, owner_col):
    n_row, n_col = lax.axis_size("row"), lax.axis_size("col")
    for bit in bits(n_col):
        block = scatter_step(block, bit, owner_col)
    for bit in bits(n_row):
        block = spread_step(block, "row", bit, owner_row)
    for bit in reversed(bits(n_col)):
        block = gather_step(block, bit)
    return block


def spread_col(x, owner_col):
    steps = bits(lax.axis_size("col"))
    x = spread_step(x, "col", steps[0], owner_col)
    half = x.shape[0] // 2
    side = lax.axis_index("col") & 1
    part = lax.dynamic_slice_in_dim(x, side * half, half, 0)
    for bit in steps[1:]:
        part = spread_step(part, "col", bit, owner_col)
    got = swap(part, "col", 1)
    a, b = pick(side == 0, part, got)
    return jnp.concatenate([a, b], 0)


def spread_row(x):
    n_row, n_col = lax.axis_size("row"), lax.axis_size("col")
    k = n_row // n_col
    row, col = lax.axis_index("row"), lax.axis_index("col")
    open_bits = n_col - 1
    for bit in reversed(bits(n_col)):
        pairs = [
            ((hi * k + lo, c), ((hi ^ bit) * k + lo, c))
            for c in range(n_col)
            for hi in range(n_col)
            for lo in range(k)
            if (hi ^ c) & open_bits == 0
        ]
        open_bits &= ~bit
        got = lax.ppermute(x, ("row", "col"), joint(pairs, n_col))
        x = jnp.where((((row // k) ^ col) & bit) == 0, x, got)
    x = x[None]
    for bit in reversed(bits(k)):
        got = swap(x, "row", bit)
        a, b = pick((row & bit) == 0, x, got)
        x = jnp.stack([a, b], 1).reshape((2 * x.shape[0],) + x.shape[1:])
    return x


def gather_rows(x):
    x = x[None]
    order = [0]
    for bit in reversed(bits(lax.axis_size("row"))):
        got = swap(x, "row", bit)
        x = jnp.concatenate([x, got], 0)
        order = order + [o ^ bit for o in order]
    return x, order


def dot32(a, b):
    ah, bh = a.astype(BF16), b.astype(BF16)
    al, bl = (a - ah.astype(F32)).astype(BF16), (b - bh.astype(F32)).astype(BF16)
    dot = functools.partial(jnp.dot, preferred_element_type=F32)
    return dot(ah, bh) + (dot(ah, bl) + dot(al, bh))


def wide(x, n):
    return jnp.broadcast_to(x, (x.shape[0], n))


def sweep_panel(t, k, lane, sub):
    n = t.shape[1]
    for j in range(0, 8, 2):
        c0, c1 = wide(t[:, k + j : k + j + 1], n), wide(t[:, k + j + 1 : k + j + 2], n)
        r0, r1 = t[j : j + 1, :], t[j + 1 : j + 2, :]
        p, q = c0[j : j + 1, :], c1[j : j + 1, :]
        q2, s = c0[j + 1 : j + 2, :], c1[j + 1 : j + 2, :]
        inv = 1.0 / (p * s - q * q2)
        on0, on1 = lane == k + j, lane == k + j + 1
        b0 = jnp.where(on0, 1.0, jnp.where(on1, 0.0, r0))
        b1 = jnp.where(on0, 0.0, jnp.where(on1, 1.0, r1))
        e0 = (s * b0 - q * b1) * inv
        e1 = (p * b1 - q2 * b0) * inv
        a0 = jnp.where(on0, e0 + 1.0, e0)
        a1 = jnp.where(on1, e1 + 1.0, e1)
        u = t - c0 * a0 - c1 * a1
        t = jnp.where(sub == j, e0, jnp.where(sub == j + 1, e1, u))
    return t


def sweep(t):
    n = t[0].shape[1]
    lane = lax.broadcasted_iota(jnp.int32, (1, n), 1)
    sub = lax.broadcasted_iota(jnp.int32, (8, n), 0)
    t = list(t)
    count = len(t)
    for at in range(count):
        k = 8 * at
        new = sweep_panel(t[at], k, lane, sub)
        inside = (lane >= k) & (lane < k + 8)
        rows = [jnp.broadcast_to(new[j : j + 1, :], (8, n)) for j in range(8)]
        for i in [(at + 1 + step) % count for step in range(count - 1)]:
            u = jnp.where(inside, 0.0, t[i])
            for j in range(8):
                u = u - wide(t[i][:, k + j : k + j + 1], n) * rows[j]
            t[i] = u
        t[at] = new
    return t


def inverse_kernel(packed_ref, high_ref, low_ref, a_ref):
    n = a_ref.shape[0]
    at = 0
    for i in range(n // TILE):
        for j in range(i + 1):
            part = packed_ref[at * TILE : (at + 1) * TILE, :]
            a_ref[i * TILE : (i + 1) * TILE, j * TILE : (j + 1) * TILE] = part
            if i != j:
                a_ref[j * TILE : (j + 1) * TILE, i * TILE : (i + 1) * TILE] = part.T
            at += 1
    eye = (
        lax.broadcasted_iota(jnp.int32, (NB, NB), 0) == lax.broadcasted_iota(jnp.int32, (NB, NB), 1)
    ).astype(F32)

    def step(k, _):
        o = pl.multiple_of(k * NB, NB)
        t = [
            a_ref[pl.ds(pl.multiple_of(o + 8 * i, 8), 8), pl.ds(o, NB)] for i in range(NB // 8)
        ]
        pivot = jnp.concatenate(sweep(t), 0)
        a_ref[pl.ds(o, NB), pl.ds(o, NB)] = eye
        new = dot32(pivot, a_ref[pl.ds(o, NB), :])

        def update(i, _):
            r = pl.multiple_of(i * TILE, TILE)
            c = a_ref[pl.ds(r, TILE), pl.ds(o, NB)]
            a_ref[pl.ds(r, TILE), pl.ds(o, NB)] = jnp.zeros((TILE, NB), F32)
            a_ref[pl.ds(r, TILE), :] = a_ref[pl.ds(r, TILE), :] - dot32(c, new)
            return 0

        lax.fori_loop(0, n // TILE, update, 0)
        a_ref[pl.ds(o, NB), :] = new
        return 0

    lax.fori_loop(0, n // NB, step, 0)

    def store(i, _):
        r = pl.multiple_of(i * NB, NB)
        a = a_ref[pl.ds(r, NB), :]
        high = a.astype(BF16)
        high_ref[pl.ds(r, NB), :] = high
        low_ref[pl.ds(r, NB), :] = (a - high.astype(F32)).astype(BF16)
        return 0

    lax.fori_loop(0, n // NB, store, 0)


def block_inverse(packed):
    shape = jax.ShapeDtypeStruct((PW, PW), BF16)
    return pl.pallas_call(
        inverse_kernel,
        out_shape=(shape, shape),
        in_specs=[pl.BlockSpec(memory_space=pltpu.VMEM)],
        out_specs=(pl.BlockSpec(memory_space=pltpu.VMEM),) * 2,
        scratch_shapes=[pltpu.VMEM((PW, PW), F32)],
        compiler_params=pltpu.CompilerParams(vmem_limit_bytes=32 << 20),
        cost_estimate=pl.CostEstimate(flops=60 * PW**3, bytes_accessed=8 * PW**2, transcendentals=0),
    )(packed)


def pack(block):
    parts = [
        block[i * TILE : (i + 1) * TILE, j * TILE : (j + 1) * TILE]
        for i in range(PW // TILE)
        for j in range(i + 1)
    ]
    return jnp.concatenate(parts, 0)


def nt(a, b):
    return lax.dot_general(a, b, (((1,), (1,)), ((), ())), preferred_element_type=F32)


def nn(a, b):
    return lax.dot_general(a, b, (((1,), (0,)), ((), ())), preferred_element_type=F32)


def shards(panels, inverse, weight, tokens, targets):
    n_row, n_col = lax.axis_size("row"), lax.axis_size("col")
    k = n_row // n_col
    row, col = lax.axis_index("row"), lax.axis_index("col")
    rows_local, cols_local = inverse.shape
    out_rows = weight.shape[0]
    token_rows = tokens.shape[0]
    anchor = panels[0] * PW
    owner_col, col_offset = anchor // cols_local, anchor % cols_local
    owner_row, row_offset = anchor // rows_local, anchor % rows_local

    block = pack(lax.dynamic_slice(inverse, (row_offset, col_offset), (PW, PW)))
    block = spread_block(block.reshape(n_col, -1, TILE), owner_row, owner_col).reshape(-1, TILE)
    high, low = block_inverse(block)

    weight_slab = lax.dynamic_slice_in_dim(weight, col_offset, PW, 1).astype(BF16)
    weight_slab = spread_col(weight_slab, owner_col)
    size = rows_local // CHUNKS
    own, across = [], []
    for i in range(CHUNKS):
        part = lax.dynamic_slice(inverse, (i * size, col_offset), (size, PW)).astype(BF16)
        part = spread_col(part, owner_col)
        own.append(part)
        across.append(spread_row(part))
    column = jnp.concatenate(own, 0)
    panel = jnp.stack(across, 1).reshape(cols_local, PW)

    all_tokens, order = gather_rows(tokens)
    all_tokens = all_tokens.reshape(-1, tokens.shape[1])

    held = []
    for i in order:
        pairs = [
            ((r, (r ^ i) // k), (r ^ i, (r ^ i) // k)) for r in range(n_row)
        ]
        tile = lax.dynamic_slice_in_dim(targets, ((row ^ i) % k) * out_rows, out_rows, 1)
        held.append(lax.ppermute(tile, ("row", "col"), joint(pairs, n_col)))
    held = jnp.concatenate(held, 0).astype(F32)

    mixed = nn(jnp.concatenate([column, column], 1), jnp.concatenate([high, low], 0))
    place = lax.broadcasted_iota(jnp.int32, mixed.shape, 0) - row_offset
    unit = (place == lax.broadcasted_iota(jnp.int32, mixed.shape, 1)).astype(F32)
    inside = (row == owner_row) & (place >= 0) & (place < PW)
    mixed = jnp.where(inside, unit, mixed).astype(BF16)

    mixed_weight = nn(
        jnp.concatenate([weight_slab, weight_slab], 1), jnp.concatenate([high, low], 0)
    ).astype(BF16)
    pruned = weight - nt(mixed_weight, panel)
    pruned_low = pruned.astype(BF16)

    value = nt(all_tokens, pruned_low) - held
    for bit in bits(n_col):
        value = value + swap(value, "col", bit)
    new_inverse = inverse - nt(mixed, panel)
    value_low = value.astype(BF16)
    correlation = lax.dot_general(
        value_low, all_tokens, (((0,), (0,)), ((), ())), preferred_element_type=F32
    ) * (1.0 / math.sqrt(token_rows * n_row))

    tiles = [jnp.zeros((token_rows, out_rows), F32)] * k
    for at, i in enumerate(order):
        pairs = [((r, r // k), (r ^ i, r // k)) for r in range(n_row)]
        tile = lax.ppermute(
            value[at * token_rows : (at + 1) * token_rows], ("row", "col"), joint(pairs, n_col)
        )
        for lo in range(k):
            tiles[lo] = tiles[lo] + jnp.where((row ^ i) % k == lo, tile, 0.0)
    residual = jnp.concatenate(tiles, 1)
    return (new_inverse, pruned, residual, correlation)


def solution(mesh):
    in_specs = (P(), P("row", "col"), P("row", "col"), P("row", "col"), P("row", "col"))
    out_specs = (P("row", "col"), P("row", "col"), P("row", "col"), P("row", "col"))
    return jax.shard_map(shards, mesh=mesh, in_specs=in_specs, out_specs=out_specs, check_vma=False)
```

```python
import functools
import math

import jax
import jax.numpy as jnp
from jax import lax
from jax.experimental import pallas as pl
from jax.experimental.pallas import tpu as pltpu
from jax.sharding import PartitionSpec as P

PW = 1024
TILE = 256
COLS = 512
ROWS = 256
NB = 128
GROUPS = 8

BF16 = jnp.bfloat16
F32 = jnp.float32


def bits(n):
    return [1 << b for b in range(n.bit_length() - 1)]


def swap(x, axis, bit):
    n = lax.axis_size(axis)
    return lax.ppermute(x, axis, [(i, i ^ bit) for i in range(n)])


def joint(pairs, cols):
    return [(a * cols + c, b * cols + d) for (a, c), (b, d) in pairs]


def pick(cond, a, b):
    return jnp.where(cond, a, b), jnp.where(cond, b, a)


def scatter(x, root, bit):
    col = lax.axis_index("col")
    mine, other = pick((col & bit) == 0, x[0::2], x[1::2])
    return jnp.where(((col ^ root) & bit) == 0, mine, swap(other, "col", bit))


def join(x, got, bit):
    a, b = pick((lax.axis_index("col") & bit) == 0, x, got)
    return jnp.stack([a, b], 1).reshape((2 * x.shape[0],) + x.shape[1:])


def rotated(d, n):
    return (d * 2) % n + d * 2 // n


def transpose_parts(x):
    n_row, n_col = lax.axis_size("row"), lax.axis_size("col")
    k = n_row // n_col
    pairs = [
        ((c * k + lo, rotated(d, n_col)), (d * k + lo, c))
        for c in range(n_col)
        for d in range(n_col)
        for lo in range(k)
    ]
    return lax.ppermute(x, ("row", "col"), joint(pairs, n_col))


def gate(*arrays):
    flat, tree = jax.tree.flatten(arrays)
    free = [pl.BlockSpec(memory_space=pl.ANY)] * len(flat)
    flat = pl.pallas_call(
        lambda *refs: None,
        out_shape=[jax.ShapeDtypeStruct(x.shape, x.dtype) for x in flat],
        in_specs=free,
        out_specs=free,
        input_output_aliases={i: i for i in range(len(flat))},
    )(*flat)
    return jax.tree.unflatten(tree, flat)


def spread_block(block, owner_row, owner_col):
    row, col = lax.axis_index("row"), lax.axis_index("col")
    col_bits, row_bits = bits(lax.axis_size("col")), bits(lax.axis_size("row"))
    for bit in col_bits:
        block = scatter(block, owner_col, bit)
    for bit in row_bits[-1:] + row_bits[:-1]:
        block = jnp.where(((row ^ owner_row) & bit) == 0, block, swap(block, "row", bit))
    for bit in reversed(col_bits):
        block = join(block, swap(block, "col", bit), bit)
    return block


def gather_rows(x):
    *near, far = bits(lax.axis_size("row"))
    parts = {0: x, far: swap(x, "row", far)}
    for root in (0, far):
        level = [root]
        for bit in reversed(near):
            parts.update({i ^ bit: swap(parts[i], "row", bit) for i in level})
            level = level + [i ^ bit for i in level]
    return parts


def assemble(parts, start):
    rows, cols = parts[0].shape
    out = jnp.zeros((rows * len(parts), cols), parts[0].dtype)
    for i, part in parts.items():
        out = lax.dynamic_update_slice_in_dim(out, part, start(lax.axis_index("row") ^ i), 0)
    return out


def dot32(a, b):
    ah, bh = a.astype(BF16), b.astype(BF16)
    al, bl = (a - ah.astype(F32)).astype(BF16), (b - bh.astype(F32)).astype(BF16)
    dot = functools.partial(jnp.dot, preferred_element_type=F32)
    return dot(ah, bh) + (dot(ah, bl) + dot(al, bh))


def wide(x, n):
    return jnp.broadcast_to(x, (x.shape[0], n))


def sweep_panel(t, k, lane, sub):
    n = t.shape[1]
    for j in range(0, 8, 2):
        c0, c1 = wide(t[:, k + j : k + j + 1], n), wide(t[:, k + j + 1 : k + j + 2], n)
        r0, r1 = t[j : j + 1, :], t[j + 1 : j + 2, :]
        p, q = c0[j : j + 1, :], c1[j : j + 1, :]
        q2, s = c0[j + 1 : j + 2, :], c1[j + 1 : j + 2, :]
        inv = 1.0 / (p * s - q * q2)
        on0, on1 = lane == k + j, lane == k + j + 1
        b0 = jnp.where(on0, 1.0, jnp.where(on1, 0.0, r0))
        b1 = jnp.where(on0, 0.0, jnp.where(on1, 1.0, r1))
        e0 = (s * b0 - q * b1) * inv
        e1 = (p * b1 - q2 * b0) * inv
        a0 = jnp.where(on0, e0 + 1.0, e0)
        a1 = jnp.where(on1, e1 + 1.0, e1)
        u = t - c0 * a0 - c1 * a1
        t = jnp.where(sub == j, e0, jnp.where(sub == j + 1, e1, u))
    return t


def sweep(t):
    n = t[0].shape[1]
    lane = lax.broadcasted_iota(jnp.int32, (1, n), 1)
    sub = lax.broadcasted_iota(jnp.int32, (8, n), 0)
    t = list(t)
    count = len(t)
    for at in range(count):
        k = 8 * at
        new = sweep_panel(t[at], k, lane, sub)
        inside = (lane >= k) & (lane < k + 8)
        rows = [jnp.broadcast_to(new[j : j + 1, :], (8, n)) for j in range(8)]
        for i in [(at + 1 + step) % count for step in range(count - 1)]:
            u = jnp.where(inside, 0.0, t[i])
            for j in range(8):
                u = u - wide(t[i][:, k + j : k + j + 1], n) * rows[j]
            t[i] = u
        t[at] = new
    return t


def inverse_kernel(first, groups, *refs):
    a_ref = refs[-1]
    n = a_ref.shape[0]
    if first == 0:
        packed_ref = refs[0]
        at = 0
        for i in range(n // TILE):
            for j in range(i + 1):
                part = packed_ref[at * TILE : (at + 1) * TILE, :]
                a_ref[i * TILE : (i + 1) * TILE, j * TILE : (j + 1) * TILE] = part
                if i != j:
                    a_ref[j * TILE : (j + 1) * TILE, i * TILE : (i + 1) * TILE] = part.T
                at += 1
    else:
        a_ref[...] = refs[0][...]
    eye = (
        lax.broadcasted_iota(jnp.int32, (NB, NB), 0) == lax.broadcasted_iota(jnp.int32, (NB, NB), 1)
    ).astype(F32)

    def step(k, _):
        o = pl.multiple_of(k * NB, NB)
        t = [
            a_ref[pl.ds(pl.multiple_of(o + 8 * i, 8), 8), pl.ds(o, NB)] for i in range(NB // 8)
        ]
        pivot = jnp.concatenate(sweep(t), 0)
        a_ref[pl.ds(o, NB), pl.ds(o, NB)] = eye
        new = dot32(pivot, a_ref[pl.ds(o, NB), :])

        def update(i, _):
            r = pl.multiple_of(i * TILE, TILE)
            c = a_ref[pl.ds(r, TILE), pl.ds(o, NB)]
            a_ref[pl.ds(r, TILE), pl.ds(o, NB)] = jnp.zeros((TILE, NB), F32)
            a_ref[pl.ds(r, TILE), :] = a_ref[pl.ds(r, TILE), :] - dot32(c, new)
            return 0

        lax.fori_loop(0, n // TILE, update, 0)
        a_ref[pl.ds(o, NB), :] = new
        return 0

    count = n // NB // groups
    lax.fori_loop(first * count, (first + 1) * count, step, 0)

    if first == groups - 1:
        high_ref, low_ref = refs[1:3]

        def store(i, _):
            r = pl.multiple_of(i * NB, NB)
            a = a_ref[pl.ds(r, NB), :]
            high = a.astype(BF16)
            high_ref[pl.ds(r, NB), :] = high
            low_ref[pl.ds(r, NB), :] = (a - high.astype(F32)).astype(BF16)
            return 0

        lax.fori_loop(0, n // NB, store, 0)


def inverse_call(first, state):
    vmem = pl.BlockSpec(memory_space=pltpu.VMEM)
    last = first == GROUPS - 1
    count = 2 if last else 1
    out = [jax.ShapeDtypeStruct((PW, PW), BF16 if last else F32)] * count
    state = pl.pallas_call(
        functools.partial(inverse_kernel, first, GROUPS),
        out_shape=out,
        in_specs=[vmem],
        out_specs=[vmem] * count,
        scratch_shapes=[pltpu.VMEM((PW, PW), F32)] if last else [],
        compiler_params=pltpu.CompilerParams(vmem_limit_bytes=24 << 20),
        cost_estimate=pl.CostEstimate(
            flops=80 * PW**3 // GROUPS, bytes_accessed=8 * PW**2, transcendentals=0
        ),
    )(state)
    return state if last else state[0]


def pack_kernel(place_ref, inverse_ref, out_ref, sems):
    row, col = pl.multiple_of(place_ref[0], TILE), pl.multiple_of(place_ref[1], TILE)
    copies = []
    for i in range(PW // TILE):
        for j in range(i + 1):
            at = len(copies)
            copies.append(
                pltpu.make_async_copy(
                    inverse_ref.at[pl.ds(row + i * TILE, TILE), pl.ds(col + j * TILE, TILE)],
                    out_ref.at[pl.ds(at * TILE, TILE), :],
                    sems.at[at],
                )
            )
    for copy in copies:
        copy.start()
    for copy in copies:
        copy.wait()


def pack(inverse, row, col):
    count = (PW // TILE) * (PW // TILE + 1) // 2
    return pl.pallas_call(
        pack_kernel,
        out_shape=jax.ShapeDtypeStruct((count * TILE, TILE), F32),
        in_specs=[pl.BlockSpec(memory_space=pltpu.SMEM), pl.BlockSpec(memory_space=pl.ANY)],
        out_specs=pl.BlockSpec(memory_space=pltpu.VMEM),
        scratch_shapes=[pltpu.SemaphoreType.DMA((count,))],
    )(jnp.stack([row, col]).astype(jnp.int32), inverse)


def nt(a, b):
    return lax.dot_general(a, b, (((1,), (1,)), ((), ())), preferred_element_type=F32)


def nn(a, b):
    return lax.dot_general(a, b, (((1,), (0,)), ((), ())), preferred_element_type=F32)


def pruned_kernel(weight_ref, mixed_ref, panel_ref, pruned_ref, pruned_low_ref):
    step = min(COLS, weight_ref.shape[1])
    for at in range(0, weight_ref.shape[1], step):
        pruned = weight_ref[:, at : at + step] - nt(mixed_ref[...], panel_ref[at : at + step, :])
        pruned_ref[:, at : at + step] = pruned
        pruned_low_ref[:, at : at + step] = pruned.astype(BF16)


def remove_from_weight(weight, mixed, panel):
    vmem = pl.BlockSpec(memory_space=pltpu.VMEM)
    rows, cols = weight.shape
    return pl.pallas_call(
        pruned_kernel,
        out_shape=(
            jax.ShapeDtypeStruct((rows, cols), F32),
            jax.ShapeDtypeStruct((rows, cols), BF16),
        ),
        in_specs=[vmem] * 3,
        out_specs=(vmem, vmem),
        compiler_params=pltpu.CompilerParams(vmem_limit_bytes=40 << 20),
        cost_estimate=pl.CostEstimate(
            flops=2 * rows * PW * cols, bytes_accessed=2 * PW * cols, transcendentals=0
        ),
    )(weight, mixed, panel)


def inverse_step_kernel(inverse_ref, mixed_ref, panel_ref, *refs):
    out_ref = refs[-1]
    step = min(COLS, inverse_ref.shape[1])
    for at in range(0, inverse_ref.shape[1], step):
        change = nt(mixed_ref[...], panel_ref[at : at + step, :])
        out_ref[:, at : at + step] = inverse_ref[:, at : at + step] - change


def remove_from_inverse(half, inverse, mixed, panel, done=None):
    vmem = pl.BlockSpec(memory_space=pltpu.VMEM)
    rows, cols = inverse.shape
    step = min(ROWS, rows // 2)
    count = rows // 2 // step
    base = half * count
    return pl.pallas_call(
        inverse_step_kernel,
        grid=(count,),
        out_shape=jax.ShapeDtypeStruct((rows, cols), F32),
        in_specs=[
            pl.BlockSpec((step, cols), lambda i: (base + i, 0)),
            pl.BlockSpec((step, PW), lambda i: (base + i, 0)),
            vmem,
        ]
        + [pl.BlockSpec(memory_space=pl.ANY)] * half,
        out_specs=pl.BlockSpec((step, cols), lambda i: (base + i, 0)),
        input_output_aliases={3: 0} if half else {},
        compiler_params=pltpu.CompilerParams(vmem_limit_bytes=52 << 20),
        cost_estimate=pl.CostEstimate(
            flops=rows * PW * cols, bytes_accessed=4 * rows * cols, transcendentals=0
        ),
    )(inverse, mixed, panel, *([done] if half else []))


def shards(panels, inverse, weight, tokens, targets):
    n_row, n_col = lax.axis_size("row"), lax.axis_size("col")
    k = n_row // n_col
    row, col = lax.axis_index("row"), lax.axis_index("col")
    rows_local, cols_local = inverse.shape
    out_rows = weight.shape[0]
    token_rows = tokens.shape[0]
    anchor = panels[0] * PW
    owner_col, col_offset = anchor // cols_local, anchor % cols_local
    owner_row, row_offset = anchor // rows_local, anchor % rows_local

    block = pack(inverse, row_offset, col_offset).reshape(n_col, -1, TILE)
    block = spread_block(block, owner_row, owner_col).reshape(-1, TILE)
    tiled = targets.reshape(token_rows, k, out_rows).swapaxes(0, 1)
    tiled = jnp.concatenate([tiled] * n_col, 0)
    state, tiled = gate(block, tiled)

    size, weight_size = rows_local // n_col, out_rows // n_col
    slab = lax.dynamic_slice_in_dim(inverse, col_offset, PW, 1).astype(BF16)
    weight_slab = lax.dynamic_slice_in_dim(weight, col_offset, PW, 1).astype(BF16)
    slab = jnp.concatenate(
        [slab.reshape(n_col, size, PW), weight_slab.reshape(n_col, weight_size, PW)], 1
    )
    for bit in bits(n_col):
        slab = scatter(slab, owner_col, bit)
    panel = gather_rows(transpose_parts(slab[0, :size]))
    panel = assemble(panel, lambda r: (r % k) * rows_local + rotated(r // k, n_col) * size)
    for bit in reversed(bits(n_col)):
        slab = join(slab, swap(slab, "col", bit), bit)
    column = slab[:, :size].reshape(rows_local, PW)
    weight_slab = slab[:, size:].reshape(out_rows, PW)

    all_tokens = assemble(gather_rows(tokens), lambda r: r * token_rows)
    value_targets = lax.all_to_all(tiled, "row", 0, 0).reshape(-1, out_rows)

    for first in range(GROUPS):
        state = inverse_call(first, state)
    high, low = state
    both = jnp.concatenate([high, low], 0)
    mixed = nn(jnp.concatenate([column, column], 1), both)
    place = lax.broadcasted_iota(jnp.int32, mixed.shape, 0) - row_offset
    unit = (place == lax.broadcasted_iota(jnp.int32, mixed.shape, 1)).astype(F32)
    inside = (row == owner_row) & (place >= 0) & (place < PW)
    mixed = jnp.where(inside, unit, mixed).astype(BF16)
    mixed_weight = nn(jnp.concatenate([weight_slab, weight_slab], 1), both).astype(BF16)

    pruned, pruned_low = remove_from_weight(weight, mixed_weight, panel)

    value_targets = jnp.where(col == row // k, value_targets.astype(F32), 0.0)
    value = nt(all_tokens, pruned_low) - value_targets
    new_inverse = remove_from_inverse(0, inverse, mixed, panel)
    for bit in bits(n_col):
        value = value + swap(value, "col", bit)
    value, new_inverse = lax.optimization_barrier((value, new_inverse))
    value_low = value.astype(BF16)
    correlation = lax.dot_general(
        value_low, all_tokens, (((0,), (0,)), ((), ())), preferred_element_type=F32
    ) * (1.0 / math.sqrt(token_rows * n_row))

    tiles = lax.all_to_all(value.reshape(n_row, token_rows, out_rows), "row", 0, 0)
    tiles = lax.dynamic_slice_in_dim(tiles, col * k, k, 0)
    residual = jnp.concatenate([tiles[lo] for lo in range(k)], 1)

    new_inverse = remove_from_inverse(1, inverse, mixed, panel, new_inverse)
    return (new_inverse, pruned, residual, correlation)


def solution(mesh):
    in_specs = (P(), P("row", "col"), P("row", "col"), P("row", "col"), P("row", "col"))
    out_specs = (P("row", "col"), P("row", "col"), P("row", "col"), P("row", "col"))
    return jax.shard_map(shards, mesh=mesh, in_specs=in_specs, out_specs=out_specs, check_vma=False)
```

```python
import functools
import math

import jax
import jax.numpy as jnp
from jax import lax
from jax.experimental import pallas as pl
from jax.experimental.pallas import tpu as pltpu
from jax.sharding import PartitionSpec as P

PW = 1024
TILE = 256
COLS = 512
ROWS = 256
NB = 128
GROUPS = 8

BF16 = jnp.bfloat16
F32 = jnp.float32


def bits(n):
    return [1 << b for b in range(n.bit_length() - 1)]


def swap(x, axis, bit):
    n = lax.axis_size(axis)
    return lax.ppermute(x, axis, [(i, i ^ bit) for i in range(n)])


def joint(pairs, cols):
    return [(a * cols + c, b * cols + d) for (a, c), (b, d) in pairs]


def pick(cond, a, b):
    return jnp.where(cond, a, b), jnp.where(cond, b, a)


def scatter(x, root, bit):
    col = lax.axis_index("col")
    mine, other = pick((col & bit) == 0, x[0::2], x[1::2])
    return jnp.where(((col ^ root) & bit) == 0, mine, swap(other, "col", bit))


def join(x, got, bit):
    a, b = pick((lax.axis_index("col") & bit) == 0, x, got)
    return jnp.stack([a, b], 1).reshape((2 * x.shape[0],) + x.shape[1:])


def rotated(d, n):
    return (d * 2) % n + d * 2 // n


def transpose_parts(x):
    n_row, n_col = lax.axis_size("row"), lax.axis_size("col")
    k = n_row // n_col
    pairs = [
        ((c * k + lo, rotated(d, n_col)), (d * k + lo, c))
        for c in range(n_col)
        for d in range(n_col)
        for lo in range(k)
    ]
    return lax.ppermute(x, ("row", "col"), joint(pairs, n_col))


def gate(*arrays):
    flat, tree = jax.tree.flatten(arrays)
    free = [pl.BlockSpec(memory_space=pl.ANY)] * len(flat)
    flat = pl.pallas_call(
        lambda *refs: None,
        out_shape=[jax.ShapeDtypeStruct(x.shape, x.dtype) for x in flat],
        in_specs=free,
        out_specs=free,
        input_output_aliases={i: i for i in range(len(flat))},
    )(*flat)
    return jax.tree.unflatten(tree, flat)


def spread_block(block, owner_row, owner_col):
    row, col = lax.axis_index("row"), lax.axis_index("col")
    col_bits, row_bits = bits(lax.axis_size("col")), bits(lax.axis_size("row"))
    for bit in col_bits:
        block = scatter(block, owner_col, bit)
    for bit in row_bits[-1:] + row_bits[:-1]:
        block = jnp.where(((row ^ owner_row) & bit) == 0, block, swap(block, "row", bit))
    for bit in reversed(col_bits):
        block = join(block, swap(block, "col", bit), bit)
    return block


def gather_rows(x):
    *near, far = bits(lax.axis_size("row"))
    parts = {0: x, far: swap(x, "row", far)}
    for root in (0, far):
        level = [root]
        for bit in reversed(near):
            parts.update({i ^ bit: swap(parts[i], "row", bit) for i in level})
            level = level + [i ^ bit for i in level]
    return parts


def assemble(parts, start):
    rows, cols = parts[0].shape
    out = jnp.zeros((rows * len(parts), cols), parts[0].dtype)
    for i, part in parts.items():
        out = lax.dynamic_update_slice_in_dim(out, part, start(lax.axis_index("row") ^ i), 0)
    return out


def terms(x):
    high = x.astype(BF16)
    return high, (x - high.astype(F32)).astype(BF16)


def left_terms(a):
    high, low = terms(a)
    return jnp.concatenate([high, low, high], 1)


def right_terms(b):
    high, low = terms(b)
    return jnp.concatenate([high, high, low], 0)


def wide(x, n):
    return jnp.broadcast_to(x, (x.shape[0], n))


def sweep_panel(t, k, lane, sub):
    n = t.shape[1]
    for j in range(0, 8, 2):
        c0, c1 = wide(t[:, k + j : k + j + 1], n), wide(t[:, k + j + 1 : k + j + 2], n)
        r0, r1 = t[j : j + 1, :], t[j + 1 : j + 2, :]
        p, q = c0[j : j + 1, :], c1[j : j + 1, :]
        q2, s = c0[j + 1 : j + 2, :], c1[j + 1 : j + 2, :]
        inv = 1.0 / (p * s - q * q2)
        on0, on1 = lane == k + j, lane == k + j + 1
        b0 = jnp.where(on0, 1.0, jnp.where(on1, 0.0, r0))
        b1 = jnp.where(on0, 0.0, jnp.where(on1, 1.0, r1))
        e0 = (s * b0 - q * b1) * inv
        e1 = (p * b1 - q2 * b0) * inv
        a0 = jnp.where(on0, e0 + 1.0, e0)
        a1 = jnp.where(on1, e1 + 1.0, e1)
        u = t - c0 * a0 - c1 * a1
        t = jnp.where(sub == j, e0, jnp.where(sub == j + 1, e1, u))
    return t


def sweep(t):
    n = t[0].shape[1]
    lane = lax.broadcasted_iota(jnp.int32, (1, n), 1)
    sub = lax.broadcasted_iota(jnp.int32, (8, n), 0)
    t = list(t)
    count = len(t)
    for at in range(count):
        k = 8 * at
        new = sweep_panel(t[at], k, lane, sub)
        inside = (lane >= k) & (lane < k + 8)
        rows = [jnp.broadcast_to(new[j : j + 1, :], (8, n)) for j in range(8)]
        for i in [(at + 1 + step) % count for step in range(count - 1)]:
            u = jnp.where(inside, 0.0, t[i])
            for j in range(8):
                u = u - wide(t[i][:, k + j : k + j + 1], n) * rows[j]
            t[i] = u
        t[at] = new
    return t


def inverse_kernel(first, groups, *refs):
    a_ref = refs[-1]
    n = a_ref.shape[0]
    if first == 0:
        packed_ref = refs[0]
        at = 0
        for i in range(n // TILE):
            for j in range(i + 1):
                part = packed_ref[at * TILE : (at + 1) * TILE, :]
                a_ref[i * TILE : (i + 1) * TILE, j * TILE : (j + 1) * TILE] = part
                if i != j:
                    a_ref[j * TILE : (j + 1) * TILE, i * TILE : (i + 1) * TILE] = part.T
                at += 1
    else:
        a_ref[...] = refs[0][...]
    eye = (
        lax.broadcasted_iota(jnp.int32, (NB, NB), 0) == lax.broadcasted_iota(jnp.int32, (NB, NB), 1)
    ).astype(F32)

    def step(k, _):
        o = pl.multiple_of(k * NB, NB)
        t = [
            a_ref[pl.ds(pl.multiple_of(o + 8 * i, 8), 8), pl.ds(o, NB)] for i in range(NB // 8)
        ]
        pivot = jnp.concatenate(sweep(t), 0)
        a_ref[pl.ds(o, NB), pl.ds(o, NB)] = eye
        new = nn(left_terms(pivot), right_terms(a_ref[pl.ds(o, NB), :]))
        right = right_terms(new)

        def update(i, _):
            r = pl.multiple_of(i * TILE, TILE)
            c = a_ref[pl.ds(r, TILE), pl.ds(o, NB)]
            a_ref[pl.ds(r, TILE), pl.ds(o, NB)] = jnp.zeros((TILE, NB), F32)
            a_ref[pl.ds(r, TILE), :] = a_ref[pl.ds(r, TILE), :] - nn(left_terms(c), right)
            return 0

        lax.fori_loop(0, n // TILE, update, 0)
        a_ref[pl.ds(o, NB), :] = new
        return 0

    count = n // NB // groups
    lax.fori_loop(first * count, (first + 1) * count, step, 0)

    if first == groups - 1:
        high_ref, low_ref = refs[1:3]

        def store(i, _):
            r = pl.multiple_of(i * NB, NB)
            a = a_ref[pl.ds(r, NB), :]
            high = a.astype(BF16)
            high_ref[pl.ds(r, NB), :] = high
            low_ref[pl.ds(r, NB), :] = (a - high.astype(F32)).astype(BF16)
            return 0

        lax.fori_loop(0, n // NB, store, 0)


def inverse_call(first, state):
    vmem = pl.BlockSpec(memory_space=pltpu.VMEM)
    last = first == GROUPS - 1
    count = 2 if last else 1
    out = [jax.ShapeDtypeStruct((PW, PW), BF16 if last else F32)] * count
    state = pl.pallas_call(
        functools.partial(inverse_kernel, first, GROUPS),
        out_shape=out,
        in_specs=[vmem],
        out_specs=[vmem] * count,
        scratch_shapes=[pltpu.VMEM((PW, PW), F32)] if last else [],
        compiler_params=pltpu.CompilerParams(vmem_limit_bytes=24 << 20),
        cost_estimate=pl.CostEstimate(
            flops=80 * PW**3 // GROUPS, bytes_accessed=8 * PW**2, transcendentals=0
        ),
    )(state)
    return state if last else state[0]


def pack_kernel(place_ref, inverse_ref, out_ref, sems):
    row, col = pl.multiple_of(place_ref[0], TILE), pl.multiple_of(place_ref[1], TILE)
    copies = []
    for i in range(PW // TILE):
        for j in range(i + 1):
            at = len(copies)
            copies.append(
                pltpu.make_async_copy(
                    inverse_ref.at[pl.ds(row + i * TILE, TILE), pl.ds(col + j * TILE, TILE)],
                    out_ref.at[pl.ds(at * TILE, TILE), :],
                    sems.at[at],
                )
            )
    for copy in copies:
        copy.start()
    for copy in copies:
        copy.wait()


def pack(inverse, row, col):
    count = (PW // TILE) * (PW // TILE + 1) // 2
    return pl.pallas_call(
        pack_kernel,
        out_shape=jax.ShapeDtypeStruct((count * TILE, TILE), F32),
        in_specs=[pl.BlockSpec(memory_space=pltpu.SMEM), pl.BlockSpec(memory_space=pl.ANY)],
        out_specs=pl.BlockSpec(memory_space=pltpu.VMEM),
        scratch_shapes=[pltpu.SemaphoreType.DMA((count,))],
    )(jnp.stack([row, col]).astype(jnp.int32), inverse)


def nt(a, b):
    return lax.dot_general(a, b, (((1,), (1,)), ((), ())), preferred_element_type=F32)


def nn(a, b):
    return lax.dot_general(a, b, (((1,), (0,)), ((), ())), preferred_element_type=F32)


def pruned_kernel(weight_ref, mixed_ref, panel_ref, pruned_ref, pruned_low_ref):
    step = min(COLS, weight_ref.shape[1])
    for at in range(0, weight_ref.shape[1], step):
        pruned = weight_ref[:, at : at + step] - nt(mixed_ref[...], panel_ref[at : at + step, :])
        pruned_ref[:, at : at + step] = pruned
        pruned_low_ref[:, at : at + step] = pruned.astype(BF16)


def remove_from_weight(weight, mixed, panel):
    vmem = pl.BlockSpec(memory_space=pltpu.VMEM)
    rows, cols = weight.shape
    return pl.pallas_call(
        pruned_kernel,
        out_shape=(
            jax.ShapeDtypeStruct((rows, cols), F32),
            jax.ShapeDtypeStruct((rows, cols), BF16),
        ),
        in_specs=[vmem] * 3,
        out_specs=(vmem, vmem),
        compiler_params=pltpu.CompilerParams(vmem_limit_bytes=40 << 20),
        cost_estimate=pl.CostEstimate(
            flops=2 * rows * PW * cols, bytes_accessed=2 * PW * cols, transcendentals=0
        ),
    )(weight, mixed, panel)


def inverse_step_kernel(inverse_ref, mixed_ref, panel_ref, *refs):
    out_ref = refs[-1]
    step = min(COLS, inverse_ref.shape[1])
    for at in range(0, inverse_ref.shape[1], step):
        change = nt(mixed_ref[...], panel_ref[at : at + step, :])
        out_ref[:, at : at + step] = inverse_ref[:, at : at + step] - change


def remove_from_inverse(half, inverse, mixed, panel, done=None):
    vmem = pl.BlockSpec(memory_space=pltpu.VMEM)
    rows, cols = inverse.shape
    step = min(ROWS, rows // 2)
    count = rows // 2 // step
    base = half * count
    return pl.pallas_call(
        inverse_step_kernel,
        grid=(count,),
        out_shape=jax.ShapeDtypeStruct((rows, cols), F32),
        in_specs=[
            pl.BlockSpec((step, cols), lambda i: (base + i, 0)),
            pl.BlockSpec((step, PW), lambda i: (base + i, 0)),
            vmem,
        ]
        + [pl.BlockSpec(memory_space=pl.ANY)] * half,
        out_specs=pl.BlockSpec((step, cols), lambda i: (base + i, 0)),
        input_output_aliases={3: 0} if half else {},
        compiler_params=pltpu.CompilerParams(vmem_limit_bytes=52 << 20),
        cost_estimate=pl.CostEstimate(
            flops=rows * PW * cols, bytes_accessed=4 * rows * cols, transcendentals=0
        ),
    )(inverse, mixed, panel, *([done] if half else []))


def shards(panels, inverse, weight, tokens, targets):
    n_row, n_col = lax.axis_size("row"), lax.axis_size("col")
    k = n_row // n_col
    row, col = lax.axis_index("row"), lax.axis_index("col")
    rows_local, cols_local = inverse.shape
    out_rows = weight.shape[0]
    token_rows = tokens.shape[0]
    anchor = panels[0] * PW
    owner_col, col_offset = anchor // cols_local, anchor % cols_local
    owner_row, row_offset = anchor // rows_local, anchor % rows_local

    block = pack(inverse, row_offset, col_offset).reshape(n_col, -1, TILE)
    block = spread_block(block, owner_row, owner_col).reshape(-1, TILE)
    tiled = targets.reshape(token_rows, k, out_rows).swapaxes(0, 1)
    tiled = jnp.concatenate([tiled] * n_col, 0)
    state, tiled = gate(block, tiled)

    size, weight_size = rows_local // n_col, out_rows // n_col
    slab = lax.dynamic_slice_in_dim(inverse, col_offset, PW, 1).astype(BF16)
    weight_slab = lax.dynamic_slice_in_dim(weight, col_offset, PW, 1).astype(BF16)
    slab = jnp.concatenate(
        [slab.reshape(n_col, size, PW), weight_slab.reshape(n_col, weight_size, PW)], 1
    )
    for bit in bits(n_col):
        slab = scatter(slab, owner_col, bit)
    panel = gather_rows(transpose_parts(slab[0, :size]))
    panel = assemble(panel, lambda r: (r % k) * rows_local + rotated(r // k, n_col) * size)
    for bit in reversed(bits(n_col)):
        slab = join(slab, swap(slab, "col", bit), bit)
    column = slab[:, :size].reshape(rows_local, PW)
    weight_slab = slab[:, size:].reshape(out_rows, PW)

    all_tokens = assemble(gather_rows(tokens), lambda r: r * token_rows)
    value_targets = lax.all_to_all(tiled, "row", 0, 0).reshape(-1, out_rows)

    for first in range(GROUPS):
        state = inverse_call(first, state)
    high, low = state
    both = jnp.concatenate([high, low], 0)
    mixed = nn(jnp.concatenate([column, column], 1), both)
    place = lax.broadcasted_iota(jnp.int32, mixed.shape, 0) - row_offset
    unit = (place == lax.broadcasted_iota(jnp.int32, mixed.shape, 1)).astype(F32)
    inside = (row == owner_row) & (place >= 0) & (place < PW)
    mixed = jnp.where(inside, unit, mixed).astype(BF16)
    mixed_weight = nn(jnp.concatenate([weight_slab, weight_slab], 1), both).astype(BF16)

    pruned, pruned_low = remove_from_weight(weight, mixed_weight, panel)

    value_targets = jnp.where(col == row // k, value_targets.astype(F32), 0.0)
    value = nt(all_tokens, pruned_low) - value_targets
    new_inverse = remove_from_inverse(0, inverse, mixed, panel)
    for bit in bits(n_col):
        value = value + swap(value, "col", bit)
    value, new_inverse = lax.optimization_barrier((value, new_inverse))
    value_low = value.astype(BF16)
    correlation = lax.dot_general(
        value_low, all_tokens, (((0,), (0,)), ((), ())), preferred_element_type=F32
    ) * (1.0 / math.sqrt(token_rows * n_row))

    tiles = lax.all_to_all(value.reshape(n_row, token_rows, out_rows), "row", 0, 0)
    tiles = lax.dynamic_slice_in_dim(tiles, col * k, k, 0)
    residual = jnp.concatenate([tiles[lo] for lo in range(k)], 1)

    new_inverse = remove_from_inverse(1, inverse, mixed, panel, new_inverse)
    return (new_inverse, pruned, residual, correlation)


def solution(mesh):
    in_specs = (P(), P("row", "col"), P("row", "col"), P("row", "col"), P("row", "col"))
    out_specs = (P("row", "col"), P("row", "col"), P("row", "col"), P("row", "col"))
    return jax.shard_map(shards, mesh=mesh, in_specs=in_specs, out_specs=out_specs, check_vma=False)
```
